512 devices in a mesh: seq: 128 (over z, y, core), head: 4 (over x).
Axes of the slice: x: 4, y: 8, z: 8, core: 2. Of those that a mesh axis runs over, the one named last changes fastest.
Arguments:
- queries: bfloat16 [65536, 1024], P('seq', 'head'), may hold values from -128 to 128
- key_tokens: bfloat16 [65536, 1024], P('seq', 'head'), may hold values from -4 to 4
- value_tokens: bfloat16 [65536, 1024], P('seq', 'head'), may hold values from -48 to 48
- norm_gain: float32 [1024], P('head'), may hold values from 0.25 to 1.75
- out_cotangent: bfloat16 [65536, 1024], P('seq', 'head'), may hold values from -6 to 6
Outputs:
- normed_out: bfloat16 [65536, 1024], P('seq', 'head')
- query_grad: bfloat16 [65536, 1024], P('seq', 'head')
- key_grad: bfloat16 [65536, 1024], P('seq', 'head')
- value_grad: bfloat16 [65536, 1024], P('seq', 'head')
The draws below stay inside these ranges and needn't reach their ends.
All inputs are finite; a program needn't handle non-finite values.
Results may differ from the reference program's by a relative error of at most 0.017.
Values may be sent and summed in bfloat16 or wider, within the bound.
A program may use at most 64 MiB of HBM per device.

```python
import jax
import jax.numpy as jnp
from jax import lax

HEADS = 8
HD = 128
LEAF = 256
LEVELS = 4
TOKENS = 65536


def paired_rows(key):
    seed_keys, seed_noise, seed_queries = jax.random.split(key, 3)
    full_width = HEADS * HD
    run_length = 2 ** (LEVELS - 1)
    run_rows = jax.random.normal(seed_keys, (TOKENS // run_length, full_width), jnp.float32)
    repeated = jnp.repeat(run_rows, run_length, axis=0)
    fresh = jax.random.normal(seed_noise, (TOKENS, full_width), jnp.float32)
    key_rows = jnp.clip(repeated + 0.3 * fresh, -4.0, 4.0)
    query_rows = jnp.clip(jax.random.normal(seed_queries, (TOKENS, full_width), jnp.float32), -4.0, 4.0)
    keys_out = key_rows
    queries_out = query_rows
    return (queries_out, keys_out)


def draw_queries(key, part):
    query_rows, key_rows = paired_rows(key)
    return query_rows.astype(jnp.bfloat16)


def draw_key_tokens(key, part):
    query_rows, key_rows = paired_rows(key)
    return key_rows.astype(jnp.bfloat16)


def draw_value_tokens(key, part):
    key = jax.random.fold_in(key, 13)
    seed_base = jax.random.fold_in(key, 0)
    full_width = HEADS * HD
    head_share = (jnp.arange(full_width, dtype=jnp.int32) // HD).astype(jnp.float32) / (HEADS - 1)
    base_rows = jnp.clip(jax.random.normal(seed_base, (TOKENS, full_width), jnp.float32), -4.0, 4.0)
    column_scale = 3.0 ** head_share
    return (base_rows * column_scale[None, :]).astype(jnp.bfloat16)


def level_of(own_key, extent, pieces, low, top_value):
    def one(axis_at, blocks):
        steps = jax.random.uniform(jax.random.fold_in(jax.random.fold_in(own_key, 6), axis_at), (blocks,), jnp.float32, low / len(pieces), top_value / len(pieces))
        return jnp.repeat(jnp.exp(steps), extent[axis_at] // blocks).reshape((-1,) + (1,) * (len(extent) - axis_at - 1))

    level = one(*pieces[0])
    for cut in pieces[1:]:
        level = level * one(*cut)
    return level


def gaussian(stream_key, dims, deviation, most, cuts=(), held_as=jnp.bfloat16):
    level = level_of(stream_key, dims, cuts, -0.22, 0.18) if cuts else 1.0
    values = jax.random.normal(stream_key, dims, jnp.float32) * deviation * level
    return jnp.minimum(jnp.maximum(values, -most), most).astype(held_as)


def setup_inputs(seed: int = 0) -> dict:
    splits = jax.random.split(jax.random.key(seed), 6)
    return {
        "queries": draw_queries(jax.random.fold_in(splits[5], 71), 0),
        "key_tokens": draw_key_tokens(jax.random.fold_in(splits[5], 71), 0),
        "value_tokens": draw_value_tokens(jax.random.fold_in(splits[5], 71), 0),
        "norm_gain": jnp.clip(1.0 + 0.15 * jax.random.normal(splits[3], (HEADS * HD,), jnp.float32), 0.25, 1.75),
        "out_cotangent": gaussian(splits[4], (TOKENS, HEADS * HD), 1.0, 6.0, ((0, 128), (1, 4))),
    }


norm_eps = 1e-06

def rounded(values_in):
    return lax.optimization_barrier(values_in.astype(jnp.bfloat16)).astype(jnp.float32)

def halve_rows(coarse):
    row_count = coarse.shape[0]
    paired = coarse.astype(jnp.float32).reshape((row_count // 2, 2) + coarse.shape[1:])
    return ((paired[:, 0] + paired[:, 1]) * 0.5).astype(jnp.bfloat16)

def swap_pairs(coarse):
    groups = coarse.shape[0]
    return coarse.reshape((groups // 2, 2) + coarse.shape[1:])[:, ::-1].reshape(coarse.shape)

def spread_rows(coarse):
    row_count = coarse.shape[0]
    return jnp.broadcast_to(0.5 * coarse[:, None], (row_count, 2) + coarse.shape[1:]).reshape((row_count * 2,) + coarse.shape[1:])

def level_count():
    count_found = 0
    for height in range(1, LEVELS + 1):
        if TOKENS // (LEAF * 2 ** (height - 1)) >= 2:
            count_found = height
    return count_found

def head_blocks(key_rows, value_rows, pyramid_depth):
    key_levels = [key_rows]
    value_levels = [value_rows]
    for height in range(2, pyramid_depth + 1):
        key_levels.append(halve_rows(key_levels[-1]))
        value_levels.append(halve_rows(value_levels[-1]))
    leaves = TOKENS // LEAF
    blocks = [(leaves, key_rows.reshape(leaves, LEAF, HD), value_rows.reshape(leaves, LEAF, HD))]
    for height in range(1, pyramid_depth + 1):
        groups = TOKENS // (LEAF * 2 ** (height - 1))
        blocks.append((groups, swap_pairs(key_levels[height - 1].reshape(groups, LEAF, HD)), swap_pairs(value_levels[height - 1].reshape(groups, LEAF, HD))))
    return blocks

def group_scores(query_rows, key_block, groups):
    grouped = query_rows.astype(jnp.float32).reshape(groups, TOKENS // groups, HD)
    return jnp.einsum('grd,gld->grl', grouped, key_block.astype(jnp.float32)) * HD ** (-0.5)

def head_forward(query_rows, key_rows, value_rows):
    blocks = head_blocks(key_rows, value_rows, level_count())
    scores = [group_scores(query_rows, entry[1], entry[0]).reshape(TOKENS, LEAF) for entry in blocks]
    row_top = lax.optimization_barrier(jnp.max(scores[0], axis=1))
    for level_scores in scores[1:]:
        row_top = jnp.maximum(row_top, lax.optimization_barrier(jnp.max(level_scores, axis=1)))
    row_total = jnp.zeros((TOKENS,), jnp.float32)
    for level_scores in scores:
        row_total = row_total + lax.optimization_barrier(jnp.sum(jnp.exp(level_scores - row_top[:, None]), axis=1))
    log_total = row_top + jnp.log(row_total)
    attn_acc = jnp.zeros((TOKENS, HD), jnp.float32)
    for entry, level_scores in zip(blocks, scores):
        groups = entry[0]
        weight = rounded(jnp.exp(level_scores - log_total[:, None]))
        attn_acc = attn_acc + jnp.einsum('grl,gld->grd', weight.reshape(groups, TOKENS // groups, LEAF), entry[2].astype(jnp.float32)).reshape(TOKENS, HD)
    return (attn_acc.astype(jnp.bfloat16), log_total)

def head_backward(query_rows, key_rows, value_rows, grad_rows, delta, log_total):
    pyramid_depth = level_count()
    blocks = head_blocks(key_rows, value_rows, pyramid_depth)
    score_scale = HD ** (-0.5)
    query_float = query_rows.astype(jnp.float32)
    grad_float = grad_rows.astype(jnp.float32)
    grad_query = jnp.zeros((TOKENS, HD), jnp.float32)
    key_cots = [jnp.zeros((TOKENS // 2 ** (height - 1), HD), jnp.float32) for height in range(1, pyramid_depth + 1)]
    value_cots = [jnp.zeros((TOKENS // 2 ** (height - 1), HD), jnp.float32) for height in range(1, pyramid_depth + 1)]
    for number in range(len(blocks)):
        groups, key_block, value_block = blocks[number]
        row_count = TOKENS // groups
        level_scores = group_scores(query_rows, key_block, groups)
        lse_view = log_total.reshape(groups, row_count, 1)
        delta_view = delta.reshape(groups, row_count, 1)
        grad_view = grad_float.reshape(groups, row_count, HD)
        query_view = query_float.reshape(groups, row_count, HD)
        probs = jnp.exp(level_scores - lse_view)
        weight = rounded(probs)
        dprob = jnp.einsum('grd,gld->grl', grad_view, value_block.astype(jnp.float32))
        dscore = rounded(probs * (dprob - delta_view))
        grad_query = grad_query + score_scale * jnp.einsum('grl,gld->grd', dscore, key_block.astype(jnp.float32)).reshape(TOKENS, HD)
        key_part = score_scale * jnp.einsum('grl,grd->gld', dscore, query_view)
        value_part = jnp.einsum('grl,grd->gld', weight, grad_view)
        if number == 0:
            key_cots[0] = key_cots[0] + key_part.reshape(TOKENS, HD)
            value_cots[0] = value_cots[0] + value_part.reshape(TOKENS, HD)
        else:
            key_cots[number - 1] = key_cots[number - 1] + swap_pairs(key_part).reshape(-1, HD)
            value_cots[number - 1] = value_cots[number - 1] + swap_pairs(value_part).reshape(-1, HD)
    for height in range(pyramid_depth, 1, -1):
        key_cots[height - 2] = key_cots[height - 2] + spread_rows(key_cots[height - 1])
        value_cots[height - 2] = value_cots[height - 2] + spread_rows(value_cots[height - 1])
    return (grad_query.astype(jnp.bfloat16), key_cots[0].astype(jnp.bfloat16), value_cots[0].astype(jnp.bfloat16))

def by_head(matrix):
    return matrix.reshape(TOKENS, HEADS, HD).transpose(1, 0, 2)

def merge_heads(stacked):
    return stacked.transpose(1, 0, 2).reshape(TOKENS, HEADS * HD)

def reference(queries, key_tokens, value_tokens, norm_gain, out_cotangent):
    query_heads = by_head(queries)
    key_heads = by_head(key_tokens)
    value_heads = by_head(value_tokens)
    attn_heads, lse_heads = lax.map(lambda packed: head_forward(packed[0], packed[1], packed[2]), (query_heads, key_heads, value_heads))
    attn_out = merge_heads(attn_heads)
    out_float = attn_out.astype(jnp.float32)
    full_width = HEADS * HD
    square = lax.optimization_barrier(jnp.sum(out_float * out_float, axis=1))
    inverse = lax.rsqrt(square / full_width + norm_eps)
    gain_float = norm_gain.astype(jnp.float32)
    normed_out = (gain_float[None, :] * out_float * inverse[:, None]).astype(jnp.bfloat16)
    scaled_cot = gain_float[None, :] * out_cotangent.astype(jnp.float32)
    inner = lax.optimization_barrier(jnp.sum(scaled_cot * out_float, axis=1))
    grad_attn = inverse[:, None] * scaled_cot - out_float * (inverse * inverse * inverse * inner / full_width)[:, None]
    grad_heads = by_head(grad_attn.astype(jnp.bfloat16))
    delta_heads = lax.optimization_barrier(jnp.sum(grad_heads.astype(jnp.float32) * attn_heads.astype(jnp.float32), axis=2))
    query_grads, key_grads, value_grads = lax.map(lambda packed: head_backward(packed[0], packed[1], packed[2], packed[3], packed[4], packed[5]), (query_heads, key_heads, value_heads, grad_heads, delta_heads, lse_heads))
    return (normed_out, merge_heads(query_grads), merge_heads(key_grads), merge_heads(value_grads))
```

```python
import functools

import jax
import jax.numpy as jnp
from jax import lax
from jax.experimental import pallas as pl
from jax.experimental.pallas import tpu as pltpu
from jax.sharding import PartitionSpec as P

HEADS = 8
LEAF = 256
NORM_EPS = 1e-06

FAR = {1: (0, 256), 2: (256, 128), 3: (384, 128), 4: (512, 64), 5: (576, 64), 6: (640, 64), 7: (704, 64)}
OWN = {1: (0, 256), 2: (256, 128), 3: (256, 128), 4: (384, 64), 5: (384, 64), 6: (384, 64), 7: (384, 64)}
LOG2E = 1.4426950408889634

NT = (((1,), (1,)), ((), ()))
NN = (((1,), (0,)), ((), ()))


def mm(a, b, dims=NN):
    return lax.dot_general(a, b, dims, preferred_element_type=jnp.float32)


def flipped(position, number):
    for bit in (1, 2, 4):
        if number & bit:
            position = position + bit - 2 * bit * ((position // bit) % 2)
    return position


def kernel(
    q_hbm, k_hbm, v_hbm, gain_ref, co_hbm,
    norm_hbm, dq_hbm, dk_hbm, dv_hbm,
    q, kv, co, coarse, cot_out, cot_in, kvt, pt, gcot, gaint, ot, gb, dqt, stats, stats_in,
    dk_acc, dv_acc, out_buf,
    in_sem, out_sem, fs, fr, bs, br, ss, sr,
):
    rows, width = q.shape
    heads = 2
    hd = 128
    full = HEADS * hd
    scale = hd ** (-0.5)
    me_seq = lax.axis_index("seq")
    me_head = lax.axis_index("head")
    n_head = 4

    loads = [
        pltpu.make_async_copy(k_hbm, kv.at[pl.ds(0, rows), pl.ds(0, width)], in_sem.at[0]),
        pltpu.make_async_copy(v_hbm, kv.at[pl.ds(0, rows), pl.ds(width, width)], in_sem.at[1]),
        pltpu.make_async_copy(q_hbm, q, in_sem.at[2]),
        pltpu.make_async_copy(co_hbm, co, in_sem.at[3]),
    ]
    for load in loads:
        load.start()

    seq_peer = {j: {"seq": flipped(me_seq, j)} for j in FAR}
    head_peer = {j: {"head": (me_head + j) % n_head} for j in (1, 2, 3)}
    barrier = pltpu.get_barrier_semaphore()
    for peer in list(seq_peer.values()) + list(head_peer.values()):
        pl.semaphore_signal(barrier, inc=1, device_id=peer, device_id_type=pl.DeviceIdType.MESH)

    r = lax.broadcasted_iota(jnp.int32, (448, rows), 0)
    c = lax.broadcasted_iota(jnp.int32, (448, rows), 1)
    low = jnp.where(r < 256, 2 * r, jnp.where(r < 384, 4 * (r - 256), 8 * (r - 384)))
    size = jnp.where(r < 256, 2, jnp.where(r < 384, 4, 8))
    weight = jnp.where(r < 256, 0.5, jnp.where(r < 384, 0.25, 0.125))
    averages = jnp.where((c >= low) & (c < low + size), weight, 0.0).astype(jnp.bfloat16)
    loads[0].wait()
    loads[1].wait()
    coarse[...] = mm(averages, kv[0:rows, :]).astype(jnp.bfloat16)

    pl.semaphore_wait(barrier, len(seq_peer) + len(head_peer))
    forward = {}
    for j in (6, 7, 4, 5, 2, 3, 1):
        (own_row, count), (far_row, _) = OWN[j], FAR[j]
        forward[j] = pltpu.make_async_remote_copy(
            src_ref=coarse.at[pl.ds(own_row, count)],
            dst_ref=kv.at[pl.ds(rows + far_row, count)],
            send_sem=fs.at[j - 1],
            recv_sem=fr.at[j - 1],
            device_id=seq_peer[j],
            device_id_type=pl.DeviceIdType.MESH,
        )
        forward[j].start()

    loads[2].wait()

    def transposed_rows(at, count):
        kvt[:, at : at + count] = kv[at : at + count, :].T

    blocks = [(0, 512), (512, 256), (768, 256), (1024, 256)]
    half = rows // 2
    m_run = {}
    l_run = {}
    m_used = {}

    def forward_block(number, h, qh):
        at, count = blocks[number]
        q_cols = slice(qh * half, (qh + 1) * half)
        q_h = q[q_cols, h * hd : (h + 1) * hd]
        s = mm(kv[at : at + count, h * hd : (h + 1) * hd], q_h, NT) * (scale * LOG2E)
        top = jnp.max(s, axis=0, keepdims=True)
        if number > 0:
            top = jnp.maximum(top, m_run[h, qh])
        p = jnp.exp2(s - top)
        total = jnp.sum(p, axis=0, keepdims=True)
        p = p.astype(jnp.bfloat16)
        pt[h, at : at + count, q_cols] = p
        o = mm(kvt[width + h * hd : width + (h + 1) * hd, at : at + count], p)
        if number > 0:
            alpha = jnp.exp2(m_run[h, qh] - top)
            total = total + l_run[h, qh] * alpha
            o = o + ot[h * hd : (h + 1) * hd, q_cols] * alpha
        ot[h * hd : (h + 1) * hd, q_cols] = o
        m_run[h, qh] = top
        l_run[h, qh] = total
        m_used[number, h, qh] = top

    transposed_rows(0, 512)
    for h in range(heads):
        for qh in range(2):
            forward_block(0, h, qh)

    loads[3].wait()
    gain = gain_ref[...]
    for h in range(heads):
        cols = slice(h * hd, (h + 1) * hd)
        gaint[cols, :] = jnp.broadcast_to(gain[:, cols], (hd, hd)).T
        gcot[cols, :] = (co[:, cols].astype(jnp.float32) * gain[:, cols]).T

    forward[1].wait_recv()
    transposed_rows(512, 256)
    for h in range(heads):
        for qh in range(2):
            forward_block(1, h, qh)
    forward[2].wait_recv()
    forward[3].wait_recv()
    transposed_rows(768, 256)
    for h in range(heads):
        for qh in range(2):
            forward_block(2, h, qh)
    for j in (4, 5, 6, 7):
        forward[j].wait_recv()
    transposed_rows(1024, 256)

    lse = {}
    stat_copies = {}
    for qh in range(2):
        q_cols = slice(qh * half, (qh + 1) * half)
        square = jnp.zeros((1, half), jnp.float32)
        inner = jnp.zeros((1, half), jnp.float32)
        for h in range(heads):
            f = slice(h * hd, (h + 1) * hd)
            forward_block(3, h, qh)
            lse[h, qh] = m_run[h, qh] + jnp.log2(l_run[h, qh])
            o = (ot[f, q_cols] * (1.0 / l_run[h, qh])).astype(jnp.bfloat16).astype(jnp.float32)
            ot[f, q_cols] = o
            square = square + jnp.sum(o * o, axis=0, keepdims=True)
            inner = inner + jnp.sum(o * gcot[f, q_cols], axis=0, keepdims=True)
        for part in range(2):
            lanes = slice(part * 128, (part + 1) * 128)
            stats[qh, part : part + 1, :] = square[:, lanes]
            stats[qh, 2 + part : 3 + part, :] = inner[:, lanes]
        for j in (1, 2, 3):
            copy = pltpu.make_async_remote_copy(
                src_ref=stats.at[qh],
                dst_ref=stats_in.at[qh, j - 1],
                send_sem=ss.at[qh, j - 1],
                recv_sem=sr.at[qh, j - 1],
                device_id=head_peer[j],
                device_id_type=pl.DeviceIdType.MESH,
            )
            copy.start()
            stat_copies[qh, j] = copy

    delta = {}
    for qh in range(2):
        q_cols = slice(qh * half, (qh + 1) * half)
        for j in (1, 2, 3):
            stat_copies[qh, j].wait_recv()
        both = stats[qh] + stats_in[qh, 0] + stats_in[qh, 1] + stats_in[qh, 2]
        square = jnp.concatenate([both[0:1], both[1:2]], axis=1)
        inner = jnp.concatenate([both[2:3], both[3:4]], axis=1)
        inverse = lax.rsqrt(square * (1.0 / full) + NORM_EPS)
        slope = inverse * inverse * inverse * inner * (1.0 / full)
        for h in range(heads):
            f = slice(h * hd, (h + 1) * hd)
            o = ot[f, q_cols]
            gain_col = gaint[f, :]
            normed = o * inverse * jnp.concatenate([gain_col] * (half // 128), axis=1)
            out_buf[0, q_cols, f] = normed.T.astype(jnp.bfloat16)
            g = (gcot[f, q_cols] * inverse - o * slope).astype(jnp.bfloat16).astype(jnp.float32)
            delta[h, qh] = jnp.sum(g * o, axis=0, keepdims=True)
            for number in range(4):
                e = jnp.exp2(m_used[number, h, qh] - lse[h, qh])
                gb[number, f, q_cols] = (g * e).astype(jnp.bfloat16)
                delta[number, h, qh] = delta[h, qh] * e
    stores = [pltpu.make_async_copy(out_buf.at[i], ref, out_sem.at[i]) for i, ref in enumerate((norm_hbm, dq_hbm, dk_hbm, dv_hbm))]
    stores[0].start()

    def backward_block(number, h):
        at, count = blocks[number]
        f = slice(h * hd, (h + 1) * hd)
        fv = slice(width + h * hd, width + (h + 1) * hd)
        g = gb[number, f, :]
        p = pt[h, at : at + count, :]
        d_row = jnp.concatenate([delta[number, h, 0], delta[number, h, 1]], axis=1)
        dp = mm(kv[at : at + count, fv], g)
        ds = (p.astype(jnp.float32) * (dp - d_row)).astype(jnp.bfloat16)
        dv = mm(p, g, NT)
        dk = mm(ds, q[:, f]) * scale
        dq = mm(kvt[f, at : at + count], ds)
        if number == 3:
            dqt[f, :] = dq
        else:
            dqt[f, :] = dqt[f, :] + dq
        if number == 0:
            dk_acc[:, f] = dk
            dv_acc[:, f] = dv
        else:
            cot_out[at - rows : at - rows + count, f] = dk.astype(jnp.bfloat16)
            cot_out[at - rows : at - rows + count, fv] = dv.astype(jnp.bfloat16)

    backward = {}

    def send_back(j):
        far_row, count = FAR[j]
        backward[j] = pltpu.make_async_remote_copy(
            src_ref=cot_out.at[pl.ds(far_row, count)],
            dst_ref=cot_in.at[pl.ds(far_row, count)],
            send_sem=bs.at[j - 1],
            recv_sem=br.at[j - 1],
            device_id=seq_peer[j],
            device_id_type=pl.DeviceIdType.MESH,
        )
        backward[j].start()

    for number, partners in ((3, (6, 7, 4, 5)), (2, (2, 3)), (1, (1,))):
        for h in range(heads):
            backward_block(number, h)
        for j in partners:
            send_back(j)
    for h in range(heads):
        backward_block(0, h)
        f = slice(h * hd, (h + 1) * hd)
        out_buf[1, :, f] = (dqt[f, :] * scale).T.astype(jnp.bfloat16)
    stores[1].start()

    def spread(count, by):
        r = lax.broadcasted_iota(jnp.int32, (rows, count), 0)
        c = lax.broadcasted_iota(jnp.int32, (rows, count), 1)
        c = c % (rows // by)
        return jnp.where((r >= by * c) & (r < by * (c + 1)), 1.0 / by, 0.0).astype(jnp.bfloat16)

    for at, by, partners in ((0, 2, (1,)), (256, 4, (2, 3)), (512, 8, (4, 5, 6, 7))):
        matrix = spread(256, by)
        for j in partners:
            backward[j].wait_recv()
        added = mm(matrix, cot_in[at : at + 256, :])
        if by < 8:
            dk_acc[...] = dk_acc[...] + added[:, :width]
            dv_acc[...] = dv_acc[...] + added[:, width:]
        else:
            out_buf[2] = (dk_acc[...] + added[:, :width]).astype(jnp.bfloat16)
            stores[2].start()
            out_buf[3] = (dv_acc[...] + added[:, width:]).astype(jnp.bfloat16)
            stores[3].start()

    for copy in list(forward.values()) + list(backward.values()) + list(stat_copies.values()):
        copy.wait_send()
    for store in stores:
        store.wait()


def on_device(queries, key_tokens, value_tokens, norm_gain, out_cotangent):
    rows, width = queries.shape
    out = jax.ShapeDtypeStruct((rows, width), jnp.bfloat16)
    bf, f32 = jnp.bfloat16, jnp.float32
    anywhere = pl.BlockSpec(memory_space=pl.ANY)
    dma = pltpu.SemaphoreType.DMA
    return pl.pallas_call(
        kernel,
        out_shape=(out, out, out, out),
        in_specs=[anywhere, anywhere, anywhere, pl.BlockSpec(memory_space=pltpu.VMEM), anywhere],
        out_specs=(anywhere,) * 4,
        scratch_shapes=[
            pltpu.VMEM((rows, width), bf),
            pltpu.VMEM((rows + 768, 2 * width), bf),
            pltpu.VMEM((rows, width), bf),
            pltpu.VMEM((448, 2 * width), bf),
            pltpu.VMEM((768, 2 * width), bf),
            pltpu.VMEM((768, 2 * width), bf),
            pltpu.VMEM((2 * width, rows + 768), bf),
            pltpu.VMEM((2, rows + 768, rows), bf),
            pltpu.VMEM((width, rows), f32),
            pltpu.VMEM((width, 128), f32),
            pltpu.VMEM((width, rows), f32),
            pltpu.VMEM((4, width, rows), bf),
            pltpu.VMEM((width, rows), f32),
            pltpu.VMEM((2, 8, 128), f32),
            pltpu.VMEM((2, 3, 8, 128), f32),
            pltpu.VMEM((rows, width), f32),
            pltpu.VMEM((rows, width), f32),
            pltpu.VMEM((4, rows, width), bf),
            dma((4,)), dma((4,)), dma((7,)), dma((7,)), dma((7,)), dma((7,)), dma((2, 3)), dma((2, 3)),
        ],
        compiler_params=pltpu.CompilerParams(
            collective_id=0, has_side_effects=True, vmem_limit_bytes=48 * 2**20
        ),
    )(queries, key_tokens, value_tokens, norm_gain.reshape(1, width), out_cotangent)


def solution(mesh):
    return jax.shard_map(
        on_device,
        mesh=mesh,
        in_specs=(P("seq", "head"), P("seq", "head"), P("seq", "head"), P("head"), P("seq", "head")),
        out_specs=(P("seq", "head"),) * 4,
        check_vma=False,
    )
```

```python
import functools

import jax
import jax.numpy as jnp
from jax import lax
from jax.experimental import pallas as pl
from jax.experimental.pallas import tpu as pltpu
from jax.sharding import PartitionSpec as P

HEADS = 8
NORM_EPS = 1e-06
LOG2E = 1.4426950408889634

LOCAL, TWIN, DIRECT, HANDED = (0, 512), (512, 256), (768, 256), (1024, 256)
LINKED = {6: (192, 64, 384), 4: (128, 64, 384), 2: (0, 128, 256)}

NT = (((1,), (1,)), ((), ()))
NN = (((1,), (0,)), ((), ()))


def mm(a, b, dims=NN):
    return lax.dot_general(a, b, dims, preferred_element_type=jnp.float32)


def flipped(position, number):
    for bit in (1, 2, 4):
        if number & bit:
            position = position + bit - 2 * bit * ((position // bit) % 2)
    return position


def kernel(
    q_hbm, k_hbm, v_hbm, gain_hbm, co_hbm,
    norm_out, dq_out, dk_out, dv_out,
    q, kv, co, gain_ref, coarse, cot_out, cot_sib, cot_send, cot_in, kvt, pt, gcot, gaint, ot, gb, dqt, stats, stats_in,
    acc,
    in_sem, fs, fr, bs, br, ss, sr,
):
    rows, width = q.shape
    hd = 128
    heads = width // hd
    full = HEADS * hd
    scale = hd ** (-0.5)
    half = rows // 2
    me_seq = lax.axis_index("seq")
    me_head = lax.axis_index("head")
    n_head = HEADS // heads

    kv_loads = []
    for h in range(heads):
        for i, ref in enumerate((k_hbm, v_hbm)):
            kv_loads.append(
                pltpu.make_async_copy(
                    ref.at[:, pl.ds(h * hd, hd)],
                    kv.at[h, pl.ds(0, rows), pl.ds(i * hd, hd)],
                    in_sem.at[2 * h + i],
                )
            )
    q_load = pltpu.make_async_copy(q_hbm, q, in_sem.at[4])
    co_load = pltpu.make_async_copy(co_hbm, co, in_sem.at[5])
    gain_load = pltpu.make_async_copy(gain_hbm, gain_ref, in_sem.at[6])
    for load in kv_loads + [q_load, co_load, gain_load]:
        load.start()

    seq_peer = {j: {"seq": flipped(me_seq, j)} for j in (1, 2, 4, 6)}
    head_peer = {j: {"head": (me_head + j) % n_head} for j in (1, 2, 3)}
    barrier = pltpu.get_barrier_semaphore()
    for peer in list(seq_peer.values()) + list(head_peer.values()):
        pl.semaphore_signal(barrier, inc=1, device_id=peer, device_id_type=pl.DeviceIdType.MESH)

    sent = []

    def send(src, dst, send_sem, recv_sem, peer):
        copy = pltpu.make_async_remote_copy(
            src_ref=src, dst_ref=dst, send_sem=send_sem, recv_sem=recv_sem,
            device_id=peer, device_id_type=pl.DeviceIdType.MESH,
        )
        copy.start()
        sent.append(copy)
        return copy

    r = lax.broadcasted_iota(jnp.int32, (448, rows), 0)
    c = lax.broadcasted_iota(jnp.int32, (448, rows), 1)
    low = jnp.where(r < 256, 2 * r, jnp.where(r < 384, 4 * (r - 256), 8 * (r - 384)))
    size = jnp.where(r < 256, 2, jnp.where(r < 384, 4, 8))
    weight = jnp.where(r < 256, 0.5, jnp.where(r < 384, 0.25, 0.125))
    averages = jnp.where((c >= low) & (c < low + size), weight, 0.0).astype(jnp.bfloat16)

    linked = {}
    twin = {}
    for h in range(heads):
        kv_loads[2 * h].wait()
        kv_loads[2 * h + 1].wait()
        coarse[h] = mm(averages, kv[h, 0:rows, :]).astype(jnp.bfloat16)
        if h == 0:
            pl.semaphore_wait(barrier, len(seq_peer) + len(head_peer))
        for i, (j, (at, count, own)) in enumerate(LINKED.items()):
            linked[h, j] = send(
                coarse.at[h, pl.ds(own, count)], kv.at[h, pl.ds(DIRECT[0] + at, count)],
                fs.at[h, i], fr.at[h, i], seq_peer[j],
            )
        twin[h] = send(
            coarse.at[h, pl.ds(0, 256)], kv.at[h, pl.ds(TWIN[0], 256)], fs.at[h, 3], fr.at[h, 3], seq_peer[1]
        )
    handed = {}

    def hand_on(h):
        for j in LINKED:
            linked[h, j].wait_recv()
        handed[h] = send(
            kv.at[h, pl.ds(DIRECT[0], 256)], kv.at[h, pl.ds(HANDED[0], 256)], fs.at[h, 4], fr.at[h, 4], seq_peer[1]
        )

    def transposed_rows(h, block):
        at, count = block
        kvt[h, :, at : at + count] = kv[h, at : at + count, :].T

    m_run, l_run, m_used = {}, {}, {}

    def forward_block(block, h, qh):
        at, count = block
        q_cols = slice(qh * half, (qh + 1) * half)
        q_h = q[q_cols, h * hd : (h + 1) * hd]
        s = mm(kv[h, at : at + count, 0:hd], q_h, NT) * (scale * LOG2E)
        top = jnp.max(s, axis=0, keepdims=True)
        first = (h, qh) not in m_run
        if not first:
            top = jnp.maximum(top, m_run[h, qh])
        p = jnp.exp2(s - top)
        total = jnp.sum(p, axis=0, keepdims=True)
        p = p.astype(jnp.bfloat16)
        pt[h, at : at + count, q_cols] = p
        o = mm(kvt[h, hd : 2 * hd, at : at + count], p)
        if not first:
            alpha = jnp.exp2(m_run[h, qh] - top)
            total = total + l_run[h, qh] * alpha
            o = o + ot[h * hd : (h + 1) * hd, q_cols] * alpha
        ot[h * hd : (h + 1) * hd, q_cols] = o
        m_run[h, qh] = top
        l_run[h, qh] = total
        m_used[block, h, qh] = top

    q_load.wait()
    for h in range(heads):
        transposed_rows(h, LOCAL)
        for qh in range(2):
            forward_block(LOCAL, h, qh)
    for h in range(heads):
        twin[h].wait_recv()
        transposed_rows(h, TWIN)
        for qh in range(2):
            forward_block(TWIN, h, qh)

    co_load.wait()
    gain_load.wait()
    gain = gain_ref[...]
    for h in range(heads):
        f = slice(h * hd, (h + 1) * hd)
        gaint[f, :] = jnp.broadcast_to(gain[:, f], (hd, hd)).T
        gcot[f, :] = (co[:, f].astype(jnp.float32) * gain[:, f]).T

    hand_on(0)
    transposed_rows(0, DIRECT)
    for qh in range(2):
        forward_block(DIRECT, 0, qh)
    handed[0].wait_recv()
    transposed_rows(0, HANDED)
    for qh in range(2):
        forward_block(HANDED, 0, qh)
    hand_on(1)
    transposed_rows(1, DIRECT)
    for qh in range(2):
        forward_block(DIRECT, 1, qh)
    handed[1].wait_recv()
    transposed_rows(1, HANDED)

    lse = {}
    stat_copies = {}
    for qh in range(2):
        q_cols = slice(qh * half, (qh + 1) * half)
        square = jnp.zeros((1, half), jnp.float32)
        inner = jnp.zeros((1, half), jnp.float32)
        forward_block(HANDED, 1, qh)
        for h in range(heads):
            f = slice(h * hd, (h + 1) * hd)
            lse[h, qh] = m_run[h, qh] + jnp.log2(l_run[h, qh])
            o = (ot[f, q_cols] * (1.0 / l_run[h, qh])).astype(jnp.bfloat16).astype(jnp.float32)
            ot[f, q_cols] = o
            square = square + jnp.sum(o * o, axis=0, keepdims=True)
            inner = inner + jnp.sum(o * gcot[f, q_cols], axis=0, keepdims=True)
        for part in range(2):
            lanes = slice(part * 128, (part + 1) * 128)
            stats[qh, part : part + 1, :] = square[:, lanes]
            stats[qh, 2 + part : 3 + part, :] = inner[:, lanes]
        for j in (2, 1, 3):
            stat_copies[qh, j] = send(
                stats.at[qh], stats_in.at[qh, j - 1], ss.at[qh, j - 1], sr.at[qh, j - 1], head_peer[j]
            )

    delta = {}
    used = (LOCAL, TWIN, DIRECT, HANDED)
    for qh in range(2):
        q_cols = slice(qh * half, (qh + 1) * half)
        for j in (1, 2, 3):
            stat_copies[qh, j].wait_recv()
        both = stats[qh] + stats_in[qh, 0] + stats_in[qh, 1] + stats_in[qh, 2]
        square = jnp.concatenate([both[0:1], both[1:2]], axis=1)
        inner = jnp.concatenate([both[2:3], both[3:4]], axis=1)
        inverse = lax.rsqrt(square * (1.0 / full) + NORM_EPS)
        slope = inverse * inverse * inverse * inner * (1.0 / full)
        for h in range(heads):
            f = slice(h * hd, (h + 1) * hd)
            o = ot[f, q_cols]
            g = (gcot[f, q_cols] * inverse - o * slope).astype(jnp.bfloat16).astype(jnp.float32)
            whole = jnp.sum(g * o, axis=0, keepdims=True)
            for number, block in enumerate(used):
                e = jnp.exp2(m_used[block, h, qh] - lse[h, qh])
                gb[number, f, q_cols] = (g * e).astype(jnp.bfloat16)
                delta[block, h, qh] = whole * e
            gcot[f, q_cols] = o * inverse * jnp.concatenate([gaint[f, :]] * (half // 128), axis=1)

    def backward_block(block, h):
        at, count = block
        f = slice(h * hd, (h + 1) * hd)
        g = gb[used.index(block), f, :]
        p = pt[h, at : at + count, :]
        d_row = jnp.concatenate([delta[block, h, 0], delta[block, h, 1]], axis=1)
        dp = mm(kv[h, at : at + count, hd : 2 * hd], g)
        ds = (p.astype(jnp.float32) * (dp - d_row)).astype(jnp.bfloat16)
        dv = mm(p, g, NT)
        dk = mm(ds, q[:, f]) * scale
        dq = mm(kvt[h, 0:hd, at : at + count], ds)
        if block == HANDED:
            dqt[f, :] = dq
        else:
            dqt[f, :] = dqt[f, :] + dq
        if block == LOCAL:
            acc[h, :, 0:hd] = dk
            acc[h, :, hd : 2 * hd] = dv
        else:
            to = at - rows
            cot_out[h, to : to + count, 0:hd] = dk.astype(jnp.bfloat16)
            cot_out[h, to : to + count, hd : 2 * hd] = dv.astype(jnp.bfloat16)

    sib, back, back_twin = {}, {}, {}

    def send_back(h):
        sib[h].wait_recv()
        mine = cot_out[h, 256:512, :].astype(jnp.float32)
        cot_send[h] = (mine + cot_sib[h].astype(jnp.float32)).astype(jnp.bfloat16)
        for i, (j, (at, count, _)) in enumerate(LINKED.items()):
            back[h, j] = send(
                cot_send.at[h, pl.ds(at, count)], cot_in.at[h, pl.ds(256 + at, count)],
                bs.at[h, i], br.at[h, i], seq_peer[j],
            )

    for h in range(heads):
        backward_block(HANDED, h)
        sib[h] = send(cot_out.at[h, pl.ds(512, 256)], cot_sib.at[h], bs.at[h, 4], br.at[h, 4], seq_peer[1])
        if h > 0:
            send_back(h - 1)
        backward_block(DIRECT, h)
    send_back(heads - 1)
    for h in range(heads):
        backward_block(TWIN, h)
        back_twin[h] = send(
            cot_out.at[h, pl.ds(0, 256)], cot_in.at[h, pl.ds(0, 256)], bs.at[h, 3], br.at[h, 3], seq_peer[1]
        )
    for h in range(heads):
        f = slice(h * hd, (h + 1) * hd)
        backward_block(LOCAL, h)
        dq_out[:, f] = (dqt[f, :] * scale).T.astype(jnp.bfloat16)
        norm_out[:, f] = gcot[f, :].T.astype(jnp.bfloat16)

    r = lax.broadcasted_iota(jnp.int32, (rows, 256), 0)
    c = lax.broadcasted_iota(jnp.int32, (rows, 256), 1)
    halves = jnp.where(r // 2 == c, 0.5, 0.0).astype(jnp.bfloat16)
    low = jnp.where(c < 128, 4 * c, 8 * ((c - 128) % 64))
    size = jnp.where(c < 128, 4, 8)
    weight = jnp.where(c < 128, 0.25, 0.125)
    others = jnp.where((r >= low) & (r < low + size), weight, 0.0).astype(jnp.bfloat16)
    for h in range(heads):
        back_twin[h].wait_recv()
        acc[h] = acc[h] + mm(halves, cot_in[h, 0:256, :])
    for h in range(heads):
        f = slice(h * hd, (h + 1) * hd)
        for j in LINKED:
            back[h, j].wait_recv()
        total = acc[h] + mm(others, cot_in[h, 256:512, :])
        dk_out[:, f] = total[:, 0:hd].astype(jnp.bfloat16)
        dv_out[:, f] = total[:, hd : 2 * hd].astype(jnp.bfloat16)

    for copy in sent:
        copy.wait_send()


def store_kernel(*refs):
    copies = [pltpu.make_async_copy(refs[i], refs[4 + i], refs[8].at[i]) for i in range(4)]
    for copy in copies:
        copy.start()
    for copy in copies:
        copy.wait()


def on_device(queries, key_tokens, value_tokens, norm_gain, out_cotangent):
    rows, width = queries.shape
    bf, f32 = jnp.bfloat16, jnp.float32
    hbm = pl.BlockSpec(memory_space=pltpu.HBM)
    vmem = pl.BlockSpec(memory_space=pltpu.VMEM)
    dma = pltpu.SemaphoreType.DMA
    in_hbm = functools.partial(pltpu.with_memory_space_constraint, memory_space=pltpu.HBM)
    in_vmem = functools.partial(pltpu.with_memory_space_constraint, memory_space=pltpu.VMEM)
    results = pl.pallas_call(
        kernel,
        out_shape=(pltpu.VMEM((rows, width), bf),) * 4,
        in_specs=[hbm] * 5,
        out_specs=(vmem,) * 4,
        scratch_shapes=[
            pltpu.VMEM((rows, width), bf),
            pltpu.VMEM((2, rows + 768, width), bf),
            pltpu.VMEM((rows, width), bf),
            pltpu.VMEM((1, width), f32),
            pltpu.VMEM((2, 448, width), bf),
            pltpu.VMEM((2, 768, width), bf),
            pltpu.VMEM((2, 256, width), bf),
            pltpu.VMEM((2, 256, width), bf),
            pltpu.VMEM((2, 512, width), bf),
            pltpu.VMEM((2, width, rows + 768), bf),
            pltpu.VMEM((2, rows + 768, rows), bf),
            pltpu.VMEM((width, rows), f32),
            pltpu.VMEM((width, 128), f32),
            pltpu.VMEM((width, rows), f32),
            pltpu.VMEM((4, width, rows), bf),
            pltpu.VMEM((width, rows), f32),
            pltpu.VMEM((2, 8, 128), f32),
            pltpu.VMEM((2, 3, 8, 128), f32),
            pltpu.VMEM((2, rows, width), f32),
            dma((7,)), dma((2, 5)), dma((2, 5)), dma((2, 5)), dma((2, 5)), dma((2, 3)), dma((2, 3)),
        ],
        compiler_params=pltpu.CompilerParams(
            collective_id=0, has_side_effects=True, vmem_limit_bytes=48 * 2**20
        ),
    )(in_hbm(queries), in_hbm(key_tokens), in_hbm(value_tokens), in_hbm(norm_gain.reshape(1, width)), in_hbm(out_cotangent))
    return pl.pallas_call(
        store_kernel,
        out_shape=(pltpu.HBM((rows, width), bf),) * 4,
        in_specs=[vmem] * 4,
        out_specs=(hbm,) * 4,
        scratch_shapes=[dma((4,))],
    )(*[in_vmem(result) for result in results])


def solution(mesh):
    return jax.shard_map(
        on_device,
        mesh=mesh,
        in_specs=(P("seq", "head"), P("seq", "head"), P("seq", "head"), P("head"), P("seq", "head")),
        out_specs=(P("seq", "head"),) * 4,
        check_vma=False,
    )
```

```python
import functools

import jax
import jax.numpy as jnp
from jax import lax
from jax.experimental import pallas as pl
from jax.experimental.pallas import tpu as pltpu
from jax.sharding import PartitionSpec as P

HEADS = 8
NORM_EPS = 1e-06
LOG2E = 1.4426950408889634

LOCAL, TWIN = (0, 512), (512, 256)
LINKED = {
    7: (448, 64, 384, 192), 6: (384, 64, 384, 192), 5: (320, 64, 384, 128), 4: (256, 64, 384, 128),
    3: (128, 128, 256, 0), 2: (0, 128, 256, 0),
}

NT = (((1,), (1,)), ((), ()))
NN = (((1,), (0,)), ((), ()))


def mm(a, b, dims=NN):
    return lax.dot_general(a, b, dims, preferred_element_type=jnp.float32)


def flipped(position, number):
    for bit in (1, 2, 4):
        if number & bit:
            position = position + bit - 2 * bit * ((position // bit) % 2)
    return position


def kernel(
    q_hbm, k_hbm, v_hbm, gain_hbm, co_hbm,
    norm_out, dq_out, dk_out, dv_out,
    near, far, near_t, far_t, given, qh, coh, gain_ref, coarse, cot_out, cot_in, pt, pf, gcot, ot, gb, dqt, stats, stats_in,
    acc, back_out, back_in, twin_cot,
    in_sem, fs, fr, bs, br, ss, sr, cs, cr,
):
    rows, width = q_hbm.shape
    hd = 128
    full = HEADS * hd
    scale = hd ** (-0.5)
    half = rows // 2
    n_head = HEADS * hd // width
    sets = (0, 1)
    me_seq = lax.axis_index("seq")
    me_head = lax.axis_index("head")
    core = me_seq % 2
    mine = pl.ds(pl.multiple_of(core * hd, hd), hd)
    other = pl.ds(pl.multiple_of((1 - core) * hd, hd), hd)

    seq_peer = {j: {"seq": flipped(me_seq, j)} for j in (7, 6, 5, 4, 3, 2, 1)}
    head_peer = {j: {"head": (me_head + j) % n_head} for j in (2, 1, 3)}
    cross_peer = {j: {**seq_peer[1], **head_peer[j]} for j in head_peer}
    peers = list(cross_peer.values()) + list(head_peer.values()) + list(seq_peer.values())
    barrier = pltpu.get_barrier_semaphore()
    for peer in peers:
        pl.semaphore_signal(barrier, inc=1, device_id=peer, device_id_type=pl.DeviceIdType.MESH)

    loads = []

    def load(src, dst):
        copy = pltpu.make_async_copy(src, dst, in_sem.at[len(loads)])
        copy.start()
        loads.append(copy)
        return copy

    kv_loads = []
    for i, ref in enumerate((k_hbm, v_hbm)):
        kv_loads.append(load(ref.at[:, mine], near.at[i, 0, pl.ds(0, rows)]))
        kv_loads.append(load(ref.at[:, other], given.at[i]))
    q_loads = [load(q_hbm.at[:, mine], qh.at[0]), load(q_hbm.at[:, other], given.at[2])]
    co_loads = [load(co_hbm.at[:, mine], coh.at[0]), load(co_hbm.at[:, other], given.at[3])]
    gain_load = load(gain_hbm, gain_ref)

    sent = []

    def send(src, dst, send_sem, recv_sem, peer):
        copy = pltpu.make_async_remote_copy(
            src_ref=src, dst_ref=dst, send_sem=send_sem, recv_sem=recv_sem,
            device_id=peer, device_id_type=pl.DeviceIdType.MESH,
        )
        copy.start()
        sent.append(copy)
        return copy

    def swap(n, src, dst):
        return send(src, dst, cs.at[n], cr.at[n], seq_peer[1])

    r = lax.broadcasted_iota(jnp.int32, (448, rows), 0)
    c = lax.broadcasted_iota(jnp.int32, (448, rows), 1)
    low = jnp.where(r < 256, 2 * r, jnp.where(r < 384, 4 * (r - 256), 8 * (r - 384)))
    size = jnp.where(r < 256, 2, jnp.where(r < 384, 4, 8))
    weight = jnp.where(r < 256, 0.5, jnp.where(r < 384, 0.25, 0.125))
    averages = jnp.where((c >= low) & (c < low + size), weight, 0.0).astype(jnp.bfloat16)

    linked = {}
    for i in range(2):
        kv_loads[2 * i].wait()
        kv_loads[2 * i + 1].wait()
        both = mm(averages, jnp.concatenate([near[i, 0, 0:rows, :], given[i]], axis=1)).astype(jnp.bfloat16)
        coarse[0, i] = both[:, 0:hd]
        coarse[1, i] = both[:, hd:]
        near[i, 1, rows : rows + 256, :] = both[0:256, 0:hd]
        if i == 0:
            pl.semaphore_wait(barrier, len(peers))
        for j, (at, count, own, _) in LINKED.items():
            linked[i, j] = send(
                coarse.at[j % 2, i, pl.ds(own, count)], far.at[i, pl.ds(at, count)],
                fs.at[i, j - 2], fr.at[i, j - 2], seq_peer[j],
            )
    for copy in q_loads + co_loads:
        copy.wait()
    swapped = [swap(i, given.at[i], near.at[i, 1, pl.ds(0, rows)]) for i in range(2)]
    swapped += [swap(2, given.at[2], qh.at[1]), swap(3, given.at[3], coh.at[1])]

    def transposed_rows(i, t, block):
        at, count = block
        near_t[i, t, :, at : at + count] = near[i, t, at : at + count, :].T

    m_run, l_run, m_used = {}, {}, {}

    def near_block(block, t, qh_at):
        at, count = block
        q_rows = slice(qh_at * half, (qh_at + 1) * half)
        s = mm(near[0, t, at : at + count, :], qh[t, q_rows, :], NT) * (scale * LOG2E)
        top = jnp.max(s, axis=0, keepdims=True)
        if block == TWIN:
            top = jnp.maximum(top, m_run[t, qh_at])
        p = jnp.exp2(s - top)
        total = jnp.sum(p, axis=0, keepdims=True)
        p = p.astype(jnp.bfloat16)
        pt[t, at : at + count, q_rows] = p
        o = mm(near_t[1, t, :, at : at + count], p)
        if block == TWIN:
            alpha = jnp.exp2(m_run[t, qh_at] - top)
            total = total + l_run[t, qh_at] * alpha
            o = o + ot[t, :, q_rows] * alpha
        ot[t, :, q_rows] = o
        m_run[t, qh_at] = top
        l_run[t, qh_at] = total
        m_used[block, t, qh_at] = top

    def near_blocks(block, t):
        transposed_rows(1, t, block)
        for qh_at in range(2):
            near_block(block, t, qh_at)

    near_blocks(LOCAL, 0)
    for copy in swapped:
        copy.wait_recv()
    for i in range(2):
        near[i, 0, rows : rows + 256, :] = mm(averages[0:256], near[i, 1, 0:rows, :]).astype(jnp.bfloat16)
    near_blocks(LOCAL, 1)
    near_blocks(TWIN, 1)
    near_blocks(TWIN, 0)

    gain_load.wait()
    gain = gain_ref[:, mine]
    gain_t = jnp.broadcast_to(gain, (hd, hd)).T
    for t in sets:
        gcot[t] = (coh[t].astype(jnp.float32) * gain).T

    for j in LINKED:
        linked[0, j].wait_recv()
    lse = {}
    for t in sets:
        m_near = jnp.concatenate([m_run[t, 0], m_run[t, 1]], axis=1)
        l_near = jnp.concatenate([l_run[t, 0], l_run[t, 1]], axis=1)
        pf[...] = mm(far[0], qh[t], NT) * (scale * LOG2E)
        top = jnp.maximum(m_near, jnp.max(pf[...], axis=0, keepdims=True))
        p = jnp.exp2(pf[...] - top)
        pf[...] = p
        total = l_near * jnp.exp2(m_near - top) + jnp.sum(p, axis=0, keepdims=True)
        lse[t] = top + jnp.log2(total)
        pt[t, 768:1280, :] = (pf[...] * (1.0 / total)).astype(jnp.bfloat16)
        ot[t] = ot[t] * jnp.exp2(m_near - lse[t])
    far_t[0] = far[0].T
    for t in sets:
        transposed_rows(0, t, LOCAL)
        transposed_rows(0, t, TWIN)

    for j in LINKED:
        linked[1, j].wait_recv()
    far_t[1] = far[1].T
    for t in sets:
        o = (ot[t] + mm(far_t[1], pt[t, 768:1280, :])).astype(jnp.bfloat16).astype(jnp.float32)
        ot[t] = o
        square = jnp.sum(o * o, axis=0, keepdims=True)
        inner = jnp.sum(o * gcot[t], axis=0, keepdims=True)
        for part in range(rows // 128):
            lanes = slice(part * 128, (part + 1) * 128)
            stats[t, part : part + 1, :] = square[:, lanes]
            stats[t, 4 + part : 5 + part, :] = inner[:, lanes]

    def send_stats(slot, peer):
        return send(stats, stats_in.at[slot], ss.at[slot], sr.at[slot], peer)

    stat_copies = [send_stats(j + 2, cross_peer[j]) for j in head_peer] + [send_stats(j - 1, head_peer[j]) for j in head_peer]
    stat_copies.append(send_stats(6, seq_peer[1]))
    for copy in stat_copies:
        copy.wait_recv()
    inverse, slope = {}, {}
    for t in sets:
        both = stats[t] + stats_in[0, t] + stats_in[1, t] + stats_in[2, t]
        both = both + (stats_in[3, 1 - t] + stats_in[4, 1 - t] + stats_in[5, 1 - t] + stats_in[6, 1 - t])
        square = jnp.concatenate([both[i : i + 1] for i in range(4)], axis=1)
        inner = jnp.concatenate([both[i : i + 1] for i in range(4, 8)], axis=1)
        inverse[t] = lax.rsqrt(square * (1.0 / full) + NORM_EPS)
        slope[t] = inverse[t] * inverse[t] * inverse[t] * inner * (1.0 / full)

    FAR_G = 2
    for t in sets:
        gb[FAR_G, t] = (gcot[t] * inverse[t] - ot[t] * slope[t]).astype(jnp.bfloat16)
    back = {}

    def send_back(i):
        for j, (at, count, _, to) in LINKED.items():
            back[i, j] = send(
                cot_out.at[i, pl.ds(at, count)], cot_in.at[j % 2, i, pl.ds(to, count)],
                bs.at[i, j - 2], br.at[i, j - 2], seq_peer[j],
            )

    cot_out[1] = (
        mm(pt[0, 768:1280, :], gb[FAR_G, 0], NT) + mm(pt[1, 768:1280, :], gb[FAR_G, 1], NT)
    ).astype(jnp.bfloat16)
    send_back(1)

    def score_cot(p, values, g, d_row):
        return (p.astype(jnp.float32) * (mm(values, g) - d_row)).astype(jnp.bfloat16)

    delta = {}
    dk = None
    for t in sets:
        g = gb[FAR_G, t]
        delta[t] = jnp.sum(g.astype(jnp.float32) * ot[t], axis=0, keepdims=True)
        ds = score_cot(pt[t, 768:1280, :], far[1], g, delta[t])
        pt[t, 768:1280, :] = ds
        part = mm(ds, qh[t])
        dk = part if dk is None else dk + part
    cot_out[0] = (dk * scale).astype(jnp.bfloat16)
    send_back(0)

    near_delta = {}
    for t in sets:
        dqt[t] = mm(far_t[0], pt[t, 768:1280, :])
        o = ot[t]
        g = gcot[t] * inverse[t] - o * slope[t]
        for n, block in enumerate((LOCAL, TWIN)):
            e = jnp.exp2(jnp.concatenate([m_used[block, t, 0], m_used[block, t, 1]], axis=1) - lse[t])
            gb[n, t] = (g * e).astype(jnp.bfloat16)
            near_delta[block, t] = delta[t] * e

    def near_cots(block, t):
        at, count = block
        g = gb[(LOCAL, TWIN).index(block), t]
        p = pt[t, at : at + count, :]
        ds = score_cot(p, near[1, t, at : at + count, :], g, near_delta[block, t])
        dqt[t] = dqt[t] + mm(near_t[0, t, :, at : at + count], ds)
        return mm(ds, qh[t]) * scale, mm(p, g, NT)

    r = lax.broadcasted_iota(jnp.int32, (rows, 256), 0)
    c = lax.broadcasted_iota(jnp.int32, (rows, 256), 1)
    halves = jnp.where(r // 2 == c, 0.5, 0.0).astype(jnp.bfloat16)
    for t in (0, 1):
        twin_k, twin_v = near_cots(TWIN, t)
        twin_cot[1 - t, :, 0:hd] = twin_k.astype(jnp.bfloat16)
        twin_cot[1 - t, :, hd:] = twin_v.astype(jnp.bfloat16)
    handed = []
    for t in (1, 0):
        local_k, local_v = near_cots(LOCAL, t)
        total = mm(halves, twin_cot[t])
        normed = (ot[t] * inverse[t] * jnp.concatenate([gain_t] * (rows // 128), axis=1)).T.astype(jnp.bfloat16)
        dq = (dqt[t] * scale).T.astype(jnp.bfloat16)
        if t == 1:
            back_out[2, :, :] = (local_k + total[:, 0:hd]).astype(jnp.bfloat16)
            back_out[3, :, :] = (local_v + total[:, hd:]).astype(jnp.bfloat16)
            back_out[0, :, :] = normed
            back_out[1, :, :] = dq
            handed.append(swap(4, back_out, back_in))
        else:
            acc[0] = local_k + total[:, 0:hd]
            acc[1] = local_v + total[:, hd:]
            norm_out[:, mine] = normed
            dq_out[:, mine] = dq
    handed[0].wait_recv()
    norm_out[:, other] = back_in[0]
    dq_out[:, other] = back_in[1]

    low = jnp.where(c < 128, 4 * c, 8 * ((c - 128) % 64))
    size = jnp.where(c < 128, 4, 8)
    weight = jnp.where(c < 128, 0.25, 0.125)
    others = jnp.where((r >= low) & (r < low + size), weight, 0.0).astype(jnp.bfloat16)
    for i, out in ((1, dv_out), (0, dk_out)):
        for j in LINKED:
            back[i, j].wait_recv()
        added = mm(others, jnp.concatenate([cot_in[0, i], cot_in[1, i]], axis=1))
        out[:, mine] = (acc[i] + added[:, 0:hd]).astype(jnp.bfloat16)
        out[:, other] = (back_in[2 + i].astype(jnp.float32) + added[:, hd:]).astype(jnp.bfloat16)

    for copy in sent:
        copy.wait_send()


def store_kernel(*refs):
    copies = [pltpu.make_async_copy(refs[i], refs[4 + i], refs[8].at[i]) for i in range(4)]
    for copy in copies:
        copy.start()
    for copy in copies:
        copy.wait()


def on_device(queries, key_tokens, value_tokens, norm_gain, out_cotangent):
    rows, width = queries.shape
    hd = 128
    bf, f32 = jnp.bfloat16, jnp.float32
    hbm = pl.BlockSpec(memory_space=pltpu.HBM)
    vmem = pl.BlockSpec(memory_space=pltpu.VMEM)
    dma = pltpu.SemaphoreType.DMA
    in_hbm = functools.partial(pltpu.with_memory_space_constraint, memory_space=pltpu.HBM)
    in_vmem = functools.partial(pltpu.with_memory_space_constraint, memory_space=pltpu.VMEM)
    results = pl.pallas_call(
        kernel,
        out_shape=(pltpu.VMEM((rows, width), bf),) * 4,
        in_specs=[hbm] * 5,
        out_specs=(vmem,) * 4,
        scratch_shapes=[
            pltpu.VMEM((2, 2, rows + 256, hd), bf),
            pltpu.VMEM((2, 512, hd), bf),
            pltpu.VMEM((2, 2, hd, rows + 256), bf),
            pltpu.VMEM((2, hd, 512), bf),
            pltpu.VMEM((4, rows, hd), bf),
            pltpu.VMEM((2, rows, hd), bf),
            pltpu.VMEM((2, rows, hd), bf),
            pltpu.VMEM((1, width), f32),
            pltpu.VMEM((2, 2, 448, hd), bf),
            pltpu.VMEM((2, 512, hd), bf),
            pltpu.VMEM((2, 2, 256, hd), bf),
            pltpu.VMEM((2, rows + 768, rows), bf),
            pltpu.VMEM((512, rows), f32),
            pltpu.VMEM((2, hd, rows), f32),
            pltpu.VMEM((2, hd, rows), f32),
            pltpu.VMEM((3, 2, hd, rows), bf),
            pltpu.VMEM((2, hd, rows), f32),
            pltpu.VMEM((2, 8, 128), f32),
            pltpu.VMEM((7, 2, 8, 128), f32),
            pltpu.VMEM((2, rows, hd), f32),
            pltpu.VMEM((4, rows, hd), bf),
            pltpu.VMEM((4, rows, hd), bf),
            pltpu.VMEM((2, 256, 2 * hd), bf),
            dma((9,)), dma((2, 6)), dma((2, 6)), dma((2, 6)), dma((2, 6)), dma((7,)), dma((7,)), dma((5,)), dma((5,)),
        ],
        compiler_params=pltpu.CompilerParams(
            collective_id=0, has_side_effects=True, vmem_limit_bytes=48 * 2**20
        ),
    )(in_hbm(queries), in_hbm(key_tokens), in_hbm(value_tokens), in_hbm(norm_gain.reshape(1, width)), in_hbm(out_cotangent))
    return pl.pallas_call(
        store_kernel,
        out_shape=(pltpu.HBM((rows, width), bf),) * 4,
        in_specs=[vmem] * 4,
        out_specs=(hbm,) * 4,
        scratch_shapes=[dma((4,))],
    )(*[in_vmem(result) for result in results])


def solution(mesh):
    return jax.shard_map(
        on_device,
        mesh=mesh,
        in_specs=(P("seq", "head"), P("seq", "head"), P("seq", "head"), P("head"), P("seq", "head")),
        out_specs=(P("seq", "head"),) * 4,
        check_vma=False,
    )
```

```python
import functools

import jax
import jax.numpy as jnp
from jax import lax
from jax.experimental import pallas as pl
from jax.experimental.pallas import tpu as pltpu
from jax.sharding import PartitionSpec as P

HEADS = 8
NORM_EPS = 1e-06
LOG2E = 1.4426950408889634

LOCAL, TWIN = (0, 512), (512, 256)
LINKED = {
    7: (448, 64, 384, 192), 6: (384, 64, 384, 192), 5: (320, 64, 384, 128), 4: (256, 64, 384, 128),
    3: (128, 128, 256, 0), 2: (0, 128, 256, 0),
}

NT = (((1,), (1,)), ((), ()))
NN = (((1,), (0,)), ((), ()))


def mm(a, b, dims=NN):
    return lax.dot_general(a, b, dims, preferred_element_type=jnp.float32)


def flipped(position, number):
    for bit in (1, 2, 4):
        if number & bit:
            position = position + bit - 2 * bit * ((position // bit) % 2)
    return position


def kernel(
    q_hbm, k_hbm, v_hbm, gain_hbm, co_hbm,
    norm_out, dq_out, dk_out, dv_out,
    near, far, near_t, far_t, given, qh, coh, gain_ref, coarse, cot_out, cot_in, pt, pf, gcot, ot, gb, dqt, stats, stats_in,
    acc, back_out, back_in, twin_cot,
    in_sem, fs, fr, bs, br, ss, sr, cs, cr, ready,
):
    rows, width = q_hbm.shape
    hd = 128
    full = HEADS * hd
    scale = hd ** (-0.5)
    half = rows // 2
    n_head = HEADS * hd // width
    sets = (0, 1)
    me_seq = lax.axis_index("seq")
    me_head = lax.axis_index("head")
    core = me_seq % 2
    mine = pl.ds(pl.multiple_of(core * hd, hd), hd)
    other = pl.ds(pl.multiple_of((1 - core) * hd, hd), hd)

    seq_peer = {j: {"seq": flipped(me_seq, j)} for j in (7, 6, 5, 4, 3, 2, 1)}
    head_peer = {j: {"head": (me_head + j) % n_head} for j in (2, 1, 3)}
    cross_peer = {j: {**seq_peer[1], **head_peer[j]} for j in head_peer}

    place = me_seq % 8
    is_lead = place == 0
    is_hub = (me_head == 0) & (core == 0)
    barrier = pltpu.get_barrier_semaphore()

    def signal(semaphore, peer):
        pl.semaphore_signal(semaphore, inc=1, device_id=peer, device_id_type=pl.DeviceIdType.MESH)

    @pl.when(jnp.logical_not(is_lead))
    def _():
        for peer in seq_peer.values():
            signal(barrier, peer)

    @pl.when(me_head != 0)
    def _():
        signal(barrier, {"seq": me_seq - core, "head": 0})

    def enter():
        pl.semaphore_wait(barrier, 6 + jnp.where(is_lead, 1, 0) + jnp.where(is_hub, 6, 0))

        @pl.when(is_lead)
        def _():
            for peer in seq_peer.values():
                signal(ready.at[0], peer)

        @pl.when(is_hub)
        def _():
            for peer in list(cross_peer.values()) + list(head_peer.values()) + [seq_peer[1]]:
                signal(ready.at[1], peer)

    loads = []

    def load(src, dst):
        copy = pltpu.make_async_copy(src, dst, in_sem.at[len(loads)])
        copy.start()
        loads.append(copy)
        return copy

    kv_loads = []
    for i, ref in enumerate((k_hbm, v_hbm)):
        kv_loads.append(load(ref.at[:, mine], near.at[i, 0, pl.ds(0, rows)]))
        kv_loads.append(load(ref.at[:, other], given.at[i]))
    q_loads = [load(q_hbm.at[:, mine], qh.at[0]), load(q_hbm.at[:, other], given.at[2])]
    co_loads = [load(co_hbm.at[:, mine], coh.at[0]), load(co_hbm.at[:, other], given.at[3])]
    gain_load = load(gain_hbm, gain_ref)

    sent = []

    def prepare(src, dst, send_sem, recv_sem, peer):
        copy = pltpu.make_async_remote_copy(
            src_ref=src, dst_ref=dst, send_sem=send_sem, recv_sem=recv_sem,
            device_id=peer, device_id_type=pl.DeviceIdType.MESH,
        )
        sent.append(copy)
        return copy

    def send(*copy_args):
        copy = prepare(*copy_args)
        copy.start()
        return copy

    def swap(n, src, dst):
        return send(src, dst, cs.at[n], cr.at[n], seq_peer[1])

    r = lax.broadcasted_iota(jnp.int32, (448, rows), 0)
    c = lax.broadcasted_iota(jnp.int32, (448, rows), 1)
    low = jnp.where(r < 256, 2 * r, jnp.where(r < 384, 4 * (r - 256), 8 * (r - 384)))
    size = jnp.where(r < 256, 2, jnp.where(r < 384, 4, 8))
    weight = jnp.where(r < 256, 0.5, jnp.where(r < 384, 0.25, 0.125))
    averages = jnp.where((c >= low) & (c < low + size), weight, 0.0).astype(jnp.bfloat16)

    linked = {}
    for i in range(2):
        kv_loads[2 * i].wait()
        kv_loads[2 * i + 1].wait()
        both = mm(averages, jnp.concatenate([near[i, 0, 0:rows, :], given[i]], axis=1)).astype(jnp.bfloat16)
        coarse[0, i] = both[:, 0:hd]
        coarse[1, i] = both[:, hd:]
        near[i, 1, rows : rows + 256, :] = both[0:256, 0:hd]
        if i == 0:
            enter()
        for j, (at, count, own, _) in LINKED.items():
            linked[i, j] = prepare(
                coarse.at[j % 2, i, pl.ds(own, count)], far.at[i, pl.ds(at, count)],
                fs.at[i, j - 2], fr.at[i, j - 2], seq_peer[j],
            )
            pl.when(place != j)(linked[i, j].start)
    for copy in q_loads + co_loads:
        copy.wait()
    swapped = []
    for n, dst in enumerate((near.at[0, 1, pl.ds(0, rows)], near.at[1, 1, pl.ds(0, rows)], qh.at[1], coh.at[1])):
        swapped.append(prepare(given.at[n], dst, cs.at[n], cr.at[n], seq_peer[1]))

    def start_swaps():
        for copy in swapped:
            copy.start()

    pl.when(place != 1)(start_swaps)

    @pl.when(jnp.logical_not(is_lead))
    def _():
        pl.semaphore_wait(ready.at[0], 1)

    for i in range(2):
        for j in LINKED:
            pl.when(place == j)(linked[i, j].start)
    pl.when(place == 1)(start_swaps)

    def transposed_rows(i, t, block):
        at, count = block
        near_t[i, t, :, at : at + count] = near[i, t, at : at + count, :].T

    m_run, l_run, m_used = {}, {}, {}

    def near_block(block, t, qh_at):
        at, count = block
        q_rows = slice(qh_at * half, (qh_at + 1) * half)
        s = mm(near[0, t, at : at + count, :], qh[t, q_rows, :], NT) * (scale * LOG2E)
        top = jnp.max(s, axis=0, keepdims=True)
        if block == TWIN:
            top = jnp.maximum(top, m_run[t, qh_at])
        p = jnp.exp2(s - top)
        total = jnp.sum(p, axis=0, keepdims=True)
        p = p.astype(jnp.bfloat16)
        pt[t, at : at + count, q_rows] = p
        o = mm(near_t[1, t, :, at : at + count], p)
        if block == TWIN:
            alpha = jnp.exp2(m_run[t, qh_at] - top)
            total = total + l_run[t, qh_at] * alpha
            o = o + ot[t, :, q_rows] * alpha
        ot[t, :, q_rows] = o
        m_run[t, qh_at] = top
        l_run[t, qh_at] = total
        m_used[block, t, qh_at] = top

    def near_blocks(block, t):
        transposed_rows(1, t, block)
        for qh_at in range(2):
            near_block(block, t, qh_at)

    near_blocks(LOCAL, 0)
    for copy in swapped:
        copy.wait_recv()
    for i in range(2):
        near[i, 0, rows : rows + 256, :] = mm(averages[0:256], near[i, 1, 0:rows, :]).astype(jnp.bfloat16)
    near_blocks(LOCAL, 1)
    near_blocks(TWIN, 1)
    near_blocks(TWIN, 0)

    gain_load.wait()
    gain = gain_ref[:, mine]
    gain_t = jnp.broadcast_to(gain, (hd, hd)).T
    for t in sets:
        gcot[t] = (coh[t].astype(jnp.float32) * gain).T

    for j in LINKED:
        linked[0, j].wait_recv()
    lse = {}
    for t in sets:
        m_near = jnp.concatenate([m_run[t, 0], m_run[t, 1]], axis=1)
        l_near = jnp.concatenate([l_run[t, 0], l_run[t, 1]], axis=1)
        pf[...] = mm(far[0], qh[t], NT) * (scale * LOG2E)
        top = jnp.maximum(m_near, jnp.max(pf[...], axis=0, keepdims=True))
        p = jnp.exp2(pf[...] - top)
        pf[...] = p
        total = l_near * jnp.exp2(m_near - top) + jnp.sum(p, axis=0, keepdims=True)
        lse[t] = top + jnp.log2(total)
        pt[t, 768:1280, :] = (pf[...] * (1.0 / total)).astype(jnp.bfloat16)
        ot[t] = ot[t] * jnp.exp2(m_near - lse[t])
    far_t[0] = far[0].T
    for t in sets:
        transposed_rows(0, t, LOCAL)
        transposed_rows(0, t, TWIN)

    for j in LINKED:
        linked[1, j].wait_recv()
    far_t[1] = far[1].T
    for t in sets:
        o = (ot[t] + mm(far_t[1], pt[t, 768:1280, :])).astype(jnp.bfloat16).astype(jnp.float32)
        ot[t] = o
        square = jnp.sum(o * o, axis=0, keepdims=True)
        inner = jnp.sum(o * gcot[t], axis=0, keepdims=True)
        for part in range(rows // 128):
            lanes = slice(part * 128, (part + 1) * 128)
            stats[t, part : part + 1, :] = square[:, lanes]
            stats[t, 4 + part : 5 + part, :] = inner[:, lanes]

    @pl.when(jnp.logical_not(is_hub))
    def _():
        pl.semaphore_wait(ready.at[1], 1)

    def send_stats(slot, peer):
        return send(stats, stats_in.at[slot], ss.at[slot], sr.at[slot], peer)

    stat_copies = [send_stats(j + 2, cross_peer[j]) for j in head_peer] + [send_stats(j - 1, head_peer[j]) for j in head_peer]
    stat_copies.append(send_stats(6, seq_peer[1]))
    for copy in stat_copies:
        copy.wait_recv()
    inverse, slope = {}, {}
    for t in sets:
        both = stats[t] + stats_in[0, t] + stats_in[1, t] + stats_in[2, t]
        both = both + (stats_in[3, 1 - t] + stats_in[4, 1 - t] + stats_in[5, 1 - t] + stats_in[6, 1 - t])
        square = jnp.concatenate([both[i : i + 1] for i in range(4)], axis=1)
        inner = jnp.concatenate([both[i : i + 1] for i in range(4, 8)], axis=1)
        inverse[t] = lax.rsqrt(square * (1.0 / full) + NORM_EPS)
        slope[t] = inverse[t] * inverse[t] * inverse[t] * inner * (1.0 / full)

    FAR_G = 2
    for t in sets:
        gb[FAR_G, t] = (gcot[t] * inverse[t] - ot[t] * slope[t]).astype(jnp.bfloat16)
    back = {}

    def send_back(i):
        for j, (at, count, _, to) in LINKED.items():
            back[i, j] = send(
                cot_out.at[i, pl.ds(at, count)], cot_in.at[j % 2, i, pl.ds(to, count)],
                bs.at[i, j - 2], br.at[i, j - 2], seq_peer[j],
            )

    cot_out[1] = (
        mm(pt[0, 768:1280, :], gb[FAR_G, 0], NT) + mm(pt[1, 768:1280, :], gb[FAR_G, 1], NT)
    ).astype(jnp.bfloat16)
    send_back(1)

    def score_cot(p, values, g, d_row):
        return (p.astype(jnp.float32) * (mm(values, g) - d_row)).astype(jnp.bfloat16)

    delta = {}
    dk = None
    for t in sets:
        g = gb[FAR_G, t]
        delta[t] = jnp.sum(g.astype(jnp.float32) * ot[t], axis=0, keepdims=True)
        ds = score_cot(pt[t, 768:1280, :], far[1], g, delta[t])
        pt[t, 768:1280, :] = ds
        part = mm(ds, qh[t])
        dk = part if dk is None else dk + part
    cot_out[0] = (dk * scale).astype(jnp.bfloat16)
    send_back(0)

    near_delta = {}
    for t in sets:
        dqt[t] = mm(far_t[0], pt[t, 768:1280, :])
        o = ot[t]
        g = gcot[t] * inverse[t] - o * slope[t]
        for n, block in enumerate((LOCAL, TWIN)):
            e = jnp.exp2(jnp.concatenate([m_used[block, t, 0], m_used[block, t, 1]], axis=1) - lse[t])
            gb[n, t] = (g * e).astype(jnp.bfloat16)
            near_delta[block, t] = delta[t] * e

    def near_cots(block, t):
        at, count = block
        g = gb[(LOCAL, TWIN).index(block), t]
        p = pt[t, at : at + count, :]
        ds = score_cot(p, near[1, t, at : at + count, :], g, near_delta[block, t])
        dqt[t] = dqt[t] + mm(near_t[0, t, :, at : at + count], ds)
        return mm(ds, qh[t]) * scale, mm(p, g, NT)

    r = lax.broadcasted_iota(jnp.int32, (rows, 256), 0)
    c = lax.broadcasted_iota(jnp.int32, (rows, 256), 1)
    halves = jnp.where(r // 2 == c, 0.5, 0.0).astype(jnp.bfloat16)
    for t in (0, 1):
        twin_k, twin_v = near_cots(TWIN, t)
        twin_cot[1 - t, :, 0:hd] = twin_k.astype(jnp.bfloat16)
        twin_cot[1 - t, :, hd:] = twin_v.astype(jnp.bfloat16)
    handed = []
    for t in (1, 0):
        local_k, local_v = near_cots(LOCAL, t)
        total = mm(halves, twin_cot[t])
        normed = (ot[t] * inverse[t] * jnp.concatenate([gain_t] * (rows // 128), axis=1)).T.astype(jnp.bfloat16)
        dq = (dqt[t] * scale).T.astype(jnp.bfloat16)
        if t == 1:
            back_out[2, :, :] = (local_k + total[:, 0:hd]).astype(jnp.bfloat16)
            back_out[3, :, :] = (local_v + total[:, hd:]).astype(jnp.bfloat16)
            back_out[0, :, :] = normed
            back_out[1, :, :] = dq
            handed.append(swap(4, back_out, back_in))
        else:
            acc[0] = local_k + total[:, 0:hd]
            acc[1] = local_v + total[:, hd:]
            norm_out[:, mine] = normed
            dq_out[:, mine] = dq
    handed[0].wait_recv()
    norm_out[:, other] = back_in[0]
    dq_out[:, other] = back_in[1]

    low = jnp.where(c < 128, 4 * c, 8 * ((c - 128) % 64))
    size = jnp.where(c < 128, 4, 8)
    weight = jnp.where(c < 128, 0.25, 0.125)
    others = jnp.where((r >= low) & (r < low + size), weight, 0.0).astype(jnp.bfloat16)
    for i, out in ((1, dv_out), (0, dk_out)):
        for j in LINKED:
            back[i, j].wait_recv()
        added = mm(others, jnp.concatenate([cot_in[0, i], cot_in[1, i]], axis=1))
        out[:, mine] = (acc[i] + added[:, 0:hd]).astype(jnp.bfloat16)
        out[:, other] = (back_in[2 + i].astype(jnp.float32) + added[:, hd:]).astype(jnp.bfloat16)

    for copy in sent:
        copy.wait_send()


def store_kernel(*refs):
    copies = [pltpu.make_async_copy(refs[i], refs[4 + i], refs[8].at[i]) for i in range(4)]
    for copy in copies:
        copy.start()
    for copy in copies:
        copy.wait()


def on_device(queries, key_tokens, value_tokens, norm_gain, out_cotangent):
    rows, width = queries.shape
    hd = 128
    bf, f32 = jnp.bfloat16, jnp.float32
    hbm = pl.BlockSpec(memory_space=pltpu.HBM)
    vmem = pl.BlockSpec(memory_space=pltpu.VMEM)
    dma = pltpu.SemaphoreType.DMA
    in_hbm = functools.partial(pltpu.with_memory_space_constraint, memory_space=pltpu.HBM)
    in_vmem = functools.partial(pltpu.with_memory_space_constraint, memory_space=pltpu.VMEM)
    results = pl.pallas_call(
        kernel,
        out_shape=(pltpu.VMEM((rows, width), bf),) * 4,
        in_specs=[hbm] * 5,
        out_specs=(vmem,) * 4,
        scratch_shapes=[
            pltpu.VMEM((2, 2, rows + 256, hd), bf),
            pltpu.VMEM((2, 512, hd), bf),
            pltpu.VMEM((2, 2, hd, rows + 256), bf),
            pltpu.VMEM((2, hd, 512), bf),
            pltpu.VMEM((4, rows, hd), bf),
            pltpu.VMEM((2, rows, hd), bf),
            pltpu.VMEM((2, rows, hd), bf),
            pltpu.VMEM((1, width), f32),
            pltpu.VMEM((2, 2, 448, hd), bf),
            pltpu.VMEM((2, 512, hd), bf),
            pltpu.VMEM((2, 2, 256, hd), bf),
            pltpu.VMEM((2, rows + 768, rows), bf),
            pltpu.VMEM((512, rows), f32),
            pltpu.VMEM((2, hd, rows), f32),
            pltpu.VMEM((2, hd, rows), f32),
            pltpu.VMEM((3, 2, hd, rows), bf),
            pltpu.VMEM((2, hd, rows), f32),
            pltpu.VMEM((2, 8, 128), f32),
            pltpu.VMEM((7, 2, 8, 128), f32),
            pltpu.VMEM((2, rows, hd), f32),
            pltpu.VMEM((4, rows, hd), bf),
            pltpu.VMEM((4, rows, hd), bf),
            pltpu.VMEM((2, 256, 2 * hd), bf),
            dma((9,)), dma((2, 6)), dma((2, 6)), dma((2, 6)), dma((2, 6)), dma((7,)), dma((7,)), dma((5,)), dma((5,)),
            pltpu.SemaphoreType.REGULAR((2,)),
        ],
        compiler_params=pltpu.CompilerParams(
            collective_id=0, has_side_effects=True, vmem_limit_bytes=48 * 2**20
        ),
    )(in_hbm(queries), in_hbm(key_tokens), in_hbm(value_tokens), in_hbm(norm_gain.reshape(1, width)), in_hbm(out_cotangent))
    return pl.pallas_call(
        store_kernel,
        out_shape=(pltpu.HBM((rows, width), bf),) * 4,
        in_specs=[vmem] * 4,
        out_specs=(hbm,) * 4,
        scratch_shapes=[dma((4,))],
    )(*[in_vmem(result) for result in results])


def solution(mesh):
    return jax.shard_map(
        on_device,
        mesh=mesh,
        in_specs=(P("seq", "head"), P("seq", "head"), P("seq", "head"), P("head"), P("seq", "head")),
        out_specs=(P("seq", "head"),) * 4,
        check_vma=False,
    )
```

```python
import functools

import jax
import jax.numpy as jnp
from jax import lax
from jax.experimental import pallas as pl
from jax.experimental.pallas import tpu as pltpu
from jax.sharding import PartitionSpec as P

HEADS = 8
NORM_EPS = 1e-06
LOG2E = 1.4426950408889634

LOCAL, TWIN = (0, 512), (512, 256)
LINKED = {
    7: (448, 64, 384, 192), 6: (384, 64, 384, 192), 5: (320, 64, 384, 128), 4: (256, 64, 384, 128),
    3: (128, 128, 256, 0), 2: (0, 128, 256, 0),
}

NT = (((1,), (1,)), ((), ()))
NN = (((1,), (0,)), ((), ()))


def mm(a, b, dims=NN):
    return lax.dot_general(a, b, dims, preferred_element_type=jnp.float32)


def flipped(position, number):
    for bit in (1, 2, 4):
        if number & bit:
            position = position + bit - 2 * bit * ((position // bit) % 2)
    return position


def kernel(
    q_hbm, k_hbm, v_hbm, gain_hbm, co_hbm,
    norm_out, dq_out, dk_out, dv_out,
    near, far, near_t, far_t, given, qh, coh, gain_ref, coarse, cot_out, cot_in, pt, pf, gcot, ot, gb, dqt, stats, stats_in,
    acc, back_out, back_in, twin_cot,
    in_sem, fs, fr, bs, br, ss, sr, cs, cr, ready,
):
    rows, width = q_hbm.shape
    hd = 128
    full = HEADS * hd
    scale = hd ** (-0.5)
    half = rows // 2
    n_head = HEADS * hd // width
    sets = (0, 1)
    me_seq = lax.axis_index("seq")
    me_head = lax.axis_index("head")
    core = me_seq % 2
    mine = pl.ds(pl.multiple_of(core * hd, hd), hd)
    other = pl.ds(pl.multiple_of((1 - core) * hd, hd), hd)

    seq_peer = {j: {"seq": flipped(me_seq, j)} for j in (7, 6, 5, 4, 3, 2, 1)}
    head_peer = {j: {"head": (me_head + j) % n_head} for j in (2, 1, 3)}
    cross_peer = {j: {**seq_peer[1], **head_peer[j]} for j in head_peer}

    place = me_seq % 8
    is_lead = place == 0
    hub_head = jnp.where(me_seq < 2, 0, 2)
    is_hub = (me_head == hub_head) & (core == 0)
    barrier = pltpu.get_barrier_semaphore()

    def signal(semaphore, peer):
        pl.semaphore_signal(semaphore, inc=1, device_id=peer, device_id_type=pl.DeviceIdType.MESH)

    @pl.when(jnp.logical_not(is_lead))
    def _():
        for peer in seq_peer.values():
            signal(barrier, peer)

    @pl.when(me_head != hub_head)
    def _():
        signal(barrier, {"seq": me_seq - core, "head": hub_head})

    def enter():
        pl.semaphore_wait(barrier, 6 + jnp.where(is_lead, 1, 0) + jnp.where(is_hub, 6, 0))

        @pl.when(is_hub)
        def _():
            for peer in list(cross_peer.values()) + list(head_peer.values()) + [seq_peer[1]]:
                signal(ready.at[1], peer)

    loads = []

    def load(src, dst):
        copy = pltpu.make_async_copy(src, dst, in_sem.at[len(loads)])
        copy.start()
        loads.append(copy)
        return copy

    kv_loads = []
    for i, ref in enumerate((k_hbm, v_hbm)):
        kv_loads.append(load(ref.at[:, mine], near.at[i, 0, pl.ds(0, rows)]))
        kv_loads.append(load(ref.at[:, other], given.at[i]))
    q_loads = [load(q_hbm.at[:, mine], qh.at[0]), load(q_hbm.at[:, other], given.at[2])]
    co_loads = [load(co_hbm.at[:, mine], coh.at[0]), load(co_hbm.at[:, other], given.at[3])]
    gain_load = load(gain_hbm, gain_ref)

    sent = []

    def prepare(src, dst, send_sem, recv_sem, peer):
        copy = pltpu.make_async_remote_copy(
            src_ref=src, dst_ref=dst, send_sem=send_sem, recv_sem=recv_sem,
            device_id=peer, device_id_type=pl.DeviceIdType.MESH,
        )
        sent.append(copy)
        return copy

    def send(*copy_args):
        copy = prepare(*copy_args)
        copy.start()
        return copy

    def swap(n, src, dst):
        return send(src, dst, cs.at[n], cr.at[n], seq_peer[1])

    @pl.when(is_lead)
    def _():
        enter()
        for peer in seq_peer.values():
            signal(ready.at[0], peer)

    r = lax.broadcasted_iota(jnp.int32, (448, rows), 0)
    c = lax.broadcasted_iota(jnp.int32, (448, rows), 1)
    low = jnp.where(r < 256, 2 * r, jnp.where(r < 384, 4 * (r - 256), 8 * (r - 384)))
    size = jnp.where(r < 256, 2, jnp.where(r < 384, 4, 8))
    weight = jnp.where(r < 256, 0.5, jnp.where(r < 384, 0.25, 0.125))
    averages = jnp.where((c >= low) & (c < low + size), weight, 0.0).astype(jnp.bfloat16)

    linked = {}
    for i in range(2):
        kv_loads[2 * i].wait()
        kv_loads[2 * i + 1].wait()
        both = mm(averages, jnp.concatenate([near[i, 0, 0:rows, :], given[i]], axis=1)).astype(jnp.bfloat16)
        coarse[0, i] = both[:, 0:hd]
        coarse[1, i] = both[:, hd:]
        near[i, 1, rows : rows + 256, :] = both[0:256, 0:hd]
        if i == 0:
            pl.when(jnp.logical_not(is_lead))(enter)
        for j, (at, count, own, _) in LINKED.items():
            linked[i, j] = prepare(
                coarse.at[j % 2, i, pl.ds(own, count)], far.at[i, pl.ds(at, count)],
                fs.at[i, j - 2], fr.at[i, j - 2], seq_peer[j],
            )
            pl.when(place != j)(linked[i, j].start)
    for copy in q_loads + co_loads:
        copy.wait()
    swapped = []
    for n, dst in ((0, near.at[0, 1, pl.ds(0, rows)]), (2, qh.at[1]), (1, near.at[1, 1, pl.ds(0, rows)]), (3, coh.at[1])):
        swapped.append(prepare(given.at[n], dst, cs.at[n], cr.at[n], seq_peer[1]))

    def start_swaps():
        for copy in swapped:
            copy.start()

    pl.when(place != 1)(start_swaps)

    @pl.when(jnp.logical_not(is_lead))
    def _():
        pl.semaphore_wait(ready.at[0], 1)

    for i in range(2):
        for j in LINKED:
            pl.when(place == j)(linked[i, j].start)
    pl.when(place == 1)(start_swaps)

    def transposed_rows(i, t, block):
        at, count = block
        near_t[i, t, :, at : at + count] = near[i, t, at : at + count, :].T

    m_run, l_run, m_used = {}, {}, {}

    def near_block(block, t, qh_at):
        at, count = block
        q_rows = slice(qh_at * half, (qh_at + 1) * half)
        s = mm(near[0, t, at : at + count, :], qh[t, q_rows, :], NT) * (scale * LOG2E)
        top = jnp.max(s, axis=0, keepdims=True)
        if block == TWIN:
            top = jnp.maximum(top, m_run[t, qh_at])
        p = jnp.exp2(s - top)
        total = jnp.sum(p, axis=0, keepdims=True)
        p = p.astype(jnp.bfloat16)
        pt[t, at : at + count, q_rows] = p
        o = mm(near_t[1, t, :, at : at + count], p)
        if block == TWIN:
            alpha = jnp.exp2(m_run[t, qh_at] - top)
            total = total + l_run[t, qh_at] * alpha
            o = o + ot[t, :, q_rows] * alpha
        ot[t, :, q_rows] = o
        m_run[t, qh_at] = top
        l_run[t, qh_at] = total
        m_used[block, t, qh_at] = top

    def near_blocks(block, t):
        transposed_rows(1, t, block)
        for qh_at in range(2):
            near_block(block, t, qh_at)

    near_blocks(LOCAL, 0)
    for copy in swapped[:3]:
        copy.wait_recv()
    for i in range(2):
        near[i, 0, rows : rows + 256, :] = mm(averages[0:256], near[i, 1, 0:rows, :]).astype(jnp.bfloat16)
    near_blocks(LOCAL, 1)
    near_blocks(TWIN, 1)
    near_blocks(TWIN, 0)

    gain_load.wait()
    swapped[3].wait_recv()
    gain = gain_ref[:, mine]
    gain_t = jnp.broadcast_to(gain, (hd, hd)).T
    for t in sets:
        gcot[t] = (coh[t].astype(jnp.float32) * gain).T

    for j in LINKED:
        linked[0, j].wait_recv()
    lse = {}
    for t in sets:
        m_near = jnp.concatenate([m_run[t, 0], m_run[t, 1]], axis=1)
        l_near = jnp.concatenate([l_run[t, 0], l_run[t, 1]], axis=1)
        pf[...] = mm(far[0], qh[t], NT) * (scale * LOG2E)
        top = jnp.maximum(m_near, jnp.max(pf[...], axis=0, keepdims=True))
        p = jnp.exp2(pf[...] - top)
        pf[...] = p
        total = l_near * jnp.exp2(m_near - top) + jnp.sum(p, axis=0, keepdims=True)
        lse[t] = top + jnp.log2(total)
        pt[t, 768:1280, :] = (pf[...] * (1.0 / total)).astype(jnp.bfloat16)
        ot[t] = ot[t] * jnp.exp2(m_near - lse[t])
    far_t[0] = far[0].T
    for t in sets:
        transposed_rows(0, t, LOCAL)
        transposed_rows(0, t, TWIN)

    for j in (7, 6, 5, 4):
        linked[1, j].wait_recv()
    far_t[1, :, 256:512] = far[1, 256:512, :].T
    for t in sets:
        ot[t] = ot[t] + mm(far_t[1, :, 256:512], pt[t, 1024:1280, :])
    for j in (3, 2):
        linked[1, j].wait_recv()
    far_t[1, :, 0:256] = far[1, 0:256, :].T
    for t in sets:
        o = (ot[t] + mm(far_t[1, :, 0:256], pt[t, 768:1024, :])).astype(jnp.bfloat16).astype(jnp.float32)
        ot[t] = o
        square = jnp.sum(o * o, axis=0, keepdims=True)
        inner = jnp.sum(o * gcot[t], axis=0, keepdims=True)
        for part in range(rows // 128):
            lanes = slice(part * 128, (part + 1) * 128)
            stats[t, part : part + 1, :] = square[:, lanes]
            stats[t, 4 + part : 5 + part, :] = inner[:, lanes]

    @pl.when(jnp.logical_not(is_hub))
    def _():
        pl.semaphore_wait(ready.at[1], 1)

    def send_stats(slot, peer):
        return send(stats, stats_in.at[slot], ss.at[slot], sr.at[slot], peer)

    stat_copies = []
    for j in head_peer:
        stat_copies += [send_stats(j + 2, cross_peer[j]), send_stats(j - 1, head_peer[j])]
    stat_copies.append(send_stats(6, seq_peer[1]))
    for copy in stat_copies:
        copy.wait_recv()
    inverse, slope = {}, {}
    for t in sets:
        both = stats[t] + stats_in[0, t] + stats_in[1, t] + stats_in[2, t]
        both = both + (stats_in[3, 1 - t] + stats_in[4, 1 - t] + stats_in[5, 1 - t] + stats_in[6, 1 - t])
        square = jnp.concatenate([both[i : i + 1] for i in range(4)], axis=1)
        inner = jnp.concatenate([both[i : i + 1] for i in range(4, 8)], axis=1)
        inverse[t] = lax.rsqrt(square * (1.0 / full) + NORM_EPS)
        slope[t] = inverse[t] * inverse[t] * inverse[t] * inner * (1.0 / full)

    FAR_G = 2
    for t in sets:
        gb[FAR_G, t] = (gcot[t] * inverse[t] - ot[t] * slope[t]).astype(jnp.bfloat16)
    back = {}

    def send_back(i, partners):
        for j in partners:
            at, count, _, to = LINKED[j]
            back[i, j] = send(
                cot_out.at[i, pl.ds(at, count)], cot_in.at[j % 2, i, pl.ds(to, count)],
                bs.at[i, j - 2], br.at[i, j - 2], seq_peer[j],
            )

    for at, partners in ((256, (7, 6, 5, 4)), (0, (3, 2))):
        p_rows = slice(768 + at, 1024 + at)
        dv = mm(pt[0, p_rows, :], gb[FAR_G, 0], NT) + mm(pt[1, p_rows, :], gb[FAR_G, 1], NT)
        cot_out[1, at : at + 256, :] = dv.astype(jnp.bfloat16)
        send_back(1, partners)

    def score_cot(p, values, g, d_row):
        return (p.astype(jnp.float32) * (mm(values, g) - d_row)).astype(jnp.bfloat16)

    delta = {}
    dk = None
    for t in sets:
        g = gb[FAR_G, t]
        delta[t] = jnp.sum(g.astype(jnp.float32) * ot[t], axis=0, keepdims=True)
        ds = score_cot(pt[t, 768:1280, :], far[1], g, delta[t])
        pt[t, 768:1280, :] = ds
        part = mm(ds, qh[t])
        dk = part if dk is None else dk + part
    cot_out[0] = (dk * scale).astype(jnp.bfloat16)
    send_back(0, LINKED)

    near_delta = {}
    for t in sets:
        dqt[t] = mm(far_t[0], pt[t, 768:1280, :])
        o = ot[t]
        g = gcot[t] * inverse[t] - o * slope[t]
        for n, block in enumerate((LOCAL, TWIN)):
            e = jnp.exp2(jnp.concatenate([m_used[block, t, 0], m_used[block, t, 1]], axis=1) - lse[t])
            gb[n, t] = (g * e).astype(jnp.bfloat16)
            near_delta[block, t] = delta[t] * e

    def near_cots(block, t):
        at, count = block
        g = gb[(LOCAL, TWIN).index(block), t]
        p = pt[t, at : at + count, :]
        ds = score_cot(p, near[1, t, at : at + count, :], g, near_delta[block, t])
        dqt[t] = dqt[t] + mm(near_t[0, t, :, at : at + count], ds)
        return mm(ds, qh[t]) * scale, mm(p, g, NT)

    r = lax.broadcasted_iota(jnp.int32, (rows, 256), 0)
    c = lax.broadcasted_iota(jnp.int32, (rows, 256), 1)
    halves = jnp.where(r // 2 == c, 0.5, 0.0).astype(jnp.bfloat16)
    for t in (0, 1):
        twin_k, twin_v = near_cots(TWIN, t)
        twin_cot[1 - t, :, 0:hd] = twin_k.astype(jnp.bfloat16)
        twin_cot[1 - t, :, hd:] = twin_v.astype(jnp.bfloat16)
    handed = []
    for t in (1, 0):
        local_k, local_v = near_cots(LOCAL, t)
        total = mm(halves, twin_cot[t])
        normed = (ot[t] * inverse[t] * jnp.concatenate([gain_t] * (rows // 128), axis=1)).T.astype(jnp.bfloat16)
        dq = (dqt[t] * scale).T.astype(jnp.bfloat16)
        if t == 1:
            back_out[2, :, :] = (local_k + total[:, 0:hd]).astype(jnp.bfloat16)
            back_out[3, :, :] = (local_v + total[:, hd:]).astype(jnp.bfloat16)
            back_out[0, :, :] = normed
            back_out[1, :, :] = dq
            handed.append(swap(4, back_out, back_in))
        else:
            acc[0] = local_k + total[:, 0:hd]
            acc[1] = local_v + total[:, hd:]
            norm_out[:, mine] = normed
            dq_out[:, mine] = dq
    handed[0].wait_recv()
    norm_out[:, other] = back_in[0]
    dq_out[:, other] = back_in[1]

    low = jnp.where(c < 128, 4 * c, 8 * ((c - 128) % 64))
    size = jnp.where(c < 128, 4, 8)
    weight = jnp.where(c < 128, 0.25, 0.125)
    others = jnp.where((r >= low) & (r < low + size), weight, 0.0).astype(jnp.bfloat16)
    for i, out in ((1, dv_out), (0, dk_out)):
        for j in LINKED:
            back[i, j].wait_recv()
        added = mm(others, jnp.concatenate([cot_in[0, i], cot_in[1, i]], axis=1))
        out[:, mine] = (acc[i] + added[:, 0:hd]).astype(jnp.bfloat16)
        out[:, other] = (back_in[2 + i].astype(jnp.float32) + added[:, hd:]).astype(jnp.bfloat16)

    for copy in sent:
        copy.wait_send()


def store_kernel(*refs):
    copies = [pltpu.make_async_copy(refs[i], refs[4 + i], refs[8].at[i]) for i in range(4)]
    for copy in copies:
        copy.start()
    for copy in copies:
        copy.wait()


def on_device(queries, key_tokens, value_tokens, norm_gain, out_cotangent):
    rows, width = queries.shape
    hd = 128
    bf, f32 = jnp.bfloat16, jnp.float32
    hbm = pl.BlockSpec(memory_space=pltpu.HBM)
    vmem = pl.BlockSpec(memory_space=pltpu.VMEM)
    dma = pltpu.SemaphoreType.DMA
    in_hbm = functools.partial(pltpu.with_memory_space_constraint, memory_space=pltpu.HBM)
    in_vmem = functools.partial(pltpu.with_memory_space_constraint, memory_space=pltpu.VMEM)
    results = pl.pallas_call(
        kernel,
        out_shape=(pltpu.VMEM((rows, width), bf),) * 4,
        in_specs=[hbm] * 5,
        out_specs=(vmem,) * 4,
        scratch_shapes=[
            pltpu.VMEM((2, 2, rows + 256, hd), bf),
            pltpu.VMEM((2, 512, hd), bf),
            pltpu.VMEM((2, 2, hd, rows + 256), bf),
            pltpu.VMEM((2, hd, 512), bf),
            pltpu.VMEM((4, rows, hd), bf),
            pltpu.VMEM((2, rows, hd), bf),
            pltpu.VMEM((2, rows, hd), bf),
            pltpu.VMEM((1, width), f32),
            pltpu.VMEM((2, 2, 448, hd), bf),
            pltpu.VMEM((2, 512, hd), bf),
            pltpu.VMEM((2, 2, 256, hd), bf),
            pltpu.VMEM((2, rows + 768, rows), bf),
            pltpu.VMEM((512, rows), f32),
            pltpu.VMEM((2, hd, rows), f32),
            pltpu.VMEM((2, hd, rows), f32),
            pltpu.VMEM((3, 2, hd, rows), bf),
            pltpu.VMEM((2, hd, rows), f32),
            pltpu.VMEM((2, 8, 128), f32),
            pltpu.VMEM((7, 2, 8, 128), f32),
            pltpu.VMEM((2, rows, hd), f32),
            pltpu.VMEM((4, rows, hd), bf),
            pltpu.VMEM((4, rows, hd), bf),
            pltpu.VMEM((2, 256, 2 * hd), bf),
            dma((9,)), dma((2, 6)), dma((2, 6)), dma((2, 6)), dma((2, 6)), dma((7,)), dma((7,)), dma((5,)), dma((5,)),
            pltpu.SemaphoreType.REGULAR((2,)),
        ],
        compiler_params=pltpu.CompilerParams(
            collective_id=0, has_side_effects=True, vmem_limit_bytes=48 * 2**20
        ),
    )(in_hbm(queries), in_hbm(key_tokens), in_hbm(value_tokens), in_hbm(norm_gain.reshape(1, width)), in_hbm(out_cotangent))
    return pl.pallas_call(
        store_kernel,
        out_shape=(pltpu.HBM((rows, width), bf),) * 4,
        in_specs=[vmem] * 4,
        out_specs=(hbm,) * 4,
        scratch_shapes=[dma((4,))],
    )(*[in_vmem(result) for result in results])


def solution(mesh):
    return jax.shard_map(
        on_device,
        mesh=mesh,
        in_specs=(P("seq", "head"), P("seq", "head"), P("seq", "head"), P("head"), P("seq", "head")),
        out_specs=(P("seq", "head"),) * 4,
        check_vma=False,
    )
```
